32 devices in a mesh: row: 4 (over y, core), col: 8 (over z, x).
Axes of the slice: x: 2, y: 2, z: 4, core: 2. Of those that a mesh axis runs over, the one named last changes fastest.
Arguments:
- sigma_top: float32 [6144, 6144], P('row', 'col')
- factor_cross: float32 [6144, 6144], P('row', 'col'), may hold values from -0.078125 to 0.078125
- factor_inverse: float32 [6144, 6144], P('row', 'col')
- block_inverse: float32 [6144, 6144], P('row', 'col')
- ancestors: int32 [12], replicated, may hold values from 0 to 23, as said below
Outputs:
- sigma_cross: float32 [6144, 6144], P('row', 'col')
- sigma_child: float32 [6144, 6144], P('row', 'col')
The draws below stay inside these ranges and needn't reach their ends.
Inputs may be any that keep to these rules, and one draw needn't show every extreme that they name: `ancestors`: 12 distinct block numbers; block 0 and block 23 are always among them.
All inputs are finite; a program needn't handle non-finite values.
Results may differ from the reference program's by a relative error of at most 0.000078.
Values sent between devices are 32-bit elements; how exact they have to be, the bound alone decides.
A program may use at most 192 MiB of HBM per device.

```python
import math
import jax
import jax.numpy as jnp
from jax import lax

ORDER = 6144
BLK = 256
NB = 24
NANC = 12


def symmetric_from(noise, key, lowest, highest):
    off_part = (noise + noise.T) * (0.70710678 / math.sqrt(ORDER))
    diagonal = jnp.exp(jax.random.uniform(key, (ORDER,), jnp.float32, math.log(lowest), math.log(highest)))
    return off_part + jnp.diag(diagonal)


def draw_sigma_top(key, part):
    first, second = jax.random.split(jax.random.fold_in(key, 11))
    noise = jax.random.normal(first, (ORDER, ORDER), jnp.float32)
    return symmetric_from(noise, second, 2.0, 6.0)


def draw_block_inverse(key, part):
    first, second = jax.random.split(jax.random.fold_in(key, 23))
    noise = jax.random.normal(first, (ORDER, ORDER), jnp.float32)
    return symmetric_from(noise, second, 1.0, 4.0)


def draw_factor_inverse(key, part):
    first, second = jax.random.split(jax.random.fold_in(key, 37))
    noise = jax.random.normal(first, (ORDER, ORDER), jnp.float32)
    diagonal = jnp.exp(jax.random.uniform(second, (ORDER,), jnp.float32, math.log(0.5), math.log(2.0)))
    return jnp.tril(noise, -1) * (1.0 / math.sqrt(ORDER)) + jnp.diag(diagonal)


def draw_ancestors(key, part):
    shuffled = jax.random.permutation(jax.random.fold_in(key, 53), NB - 2).astype(jnp.int32) + 1
    ends = jnp.array([0, NB - 1], dtype=jnp.int32)
    return jnp.concatenate([ends, shuffled[:NANC - 2]]).astype(jnp.int32)


def block_levels(rng, extent, cuts, smallest, largest):
    level, own = 1.0, jax.random.fold_in(rng, 6)
    for axis_at, blocks in cuts:
        draws = jnp.exp(jax.random.uniform(jax.random.fold_in(own, axis_at), (blocks,), jnp.float32, smallest / len(cuts), largest / len(cuts)))
        level = level * jnp.repeat(draws, extent[axis_at] // blocks).reshape([-1 if axis == axis_at else 1 for axis in range(len(extent))])
    return level


def bell_draw(rng, dims, spread, bound, cuts=(), kind=jnp.bfloat16):
    values = jax.random.normal(rng, dims, jnp.float32) * spread
    if len(cuts) > 0:
        values = block_levels(rng, dims, cuts, -0.22, 0.18) * values
    return jnp.clip(values, min=-bound, max=bound).astype(kind)


def setup_inputs(seed: int = 0) -> dict:
    streams_of = jax.random.split(jax.random.key(seed), 6)
    sigma_top = draw_sigma_top(jax.random.fold_in(streams_of[5], 71), 0)
    factor_cross = bell_draw(streams_of[1], (ORDER, ORDER), ORDER ** -0.5, 0.078125, ((0, 4), (1, 8)), jnp.float32)
    factor_inverse = draw_factor_inverse(jax.random.fold_in(streams_of[5], 71), 0)
    block_inverse = draw_block_inverse(jax.random.fold_in(streams_of[5], 71), 0)
    ancestors = draw_ancestors(jax.random.fold_in(streams_of[5], 71), 0)
    return dict(sigma_top=sigma_top, factor_cross=factor_cross, factor_inverse=factor_inverse, block_inverse=block_inverse, ancestors=ancestors)


def reference(sigma_top, factor_cross, factor_inverse, block_inverse, ancestors):
    blocks = jnp.arange(ORDER, dtype=jnp.int32) // BLK
    living = jnp.any(blocks[:, None] == ancestors[None, :], axis=1)
    masked = jnp.where(living[:, None], factor_cross, jnp.float32(0.0))
    update = jnp.dot(masked, factor_inverse, precision=lax.Precision.HIGHEST, preferred_element_type=jnp.float32)
    product = jnp.dot(sigma_top, update, precision=lax.Precision.HIGHEST, preferred_element_type=jnp.float32)
    sigma_cross = jnp.where(living[:, None], -product, jnp.float32(0.0))
    correction = jnp.dot(update.T, sigma_cross, precision=lax.Precision.HIGHEST, preferred_element_type=jnp.float32)
    sigma_child = block_inverse - correction
    return sigma_cross, sigma_child
```

```python
import functools

import jax
import jax.numpy as jnp
from jax import lax
from jax.experimental import pallas as pl
from jax.experimental.pallas import tpu as pltpu
from jax.sharding import PartitionSpec as P

BLK = 256
CHIPS_Z = 4


def gather_kernel(nz, nx, own_ref, out_ref, send_sem, recv_sem, local_sem):
    col = lax.axis_index("col")
    z, x = col // nx, col % nx
    width = own_ref.shape[1]
    up, down, right, left = 0, 1, 2, 3
    step = {up: nx, down: -nx, right: 1, left: -1}
    exists = {up: z < nz - 1, down: z > 0, right: x < nx - 1, left: x > 0}

    def place(block):
        return out_ref.at[:, pl.ds(pl.multiple_of(block * width, 128), width)]

    def copy(block, way, own=False):
        return pltpu.make_async_remote_copy(
            src_ref=own_ref if own else place(block),
            dst_ref=place(block),
            send_sem=send_sem.at[way, block],
            recv_sem=recv_sem.at[block],
            device_id={"col": col + step[way]},
            device_id_type=pl.DeviceIdType.MESH,
        )

    def walk(on_arrival, act):
        for way in (up, down, right, left):
            pl.when(exists[way])(functools.partial(act, col, way, True))
        for hop in range(1, nz):
            for way, there in ((up, z - hop >= 0), (down, z + hop < nz)):
                block = col - hop * step[way]

                @pl.when(there)
                def _(block=block, way=way):
                    on_arrival(block, way)
                    for onward in (way, right, left):
                        pl.when(exists[onward])(functools.partial(act, block, onward, False))

        for hop in range(1, nx):
            for line in range(nz):
                for way, there in ((right, x - hop >= 0), (left, x + hop < nx)):
                    block = lax.rem(z + line, nz) * nx + x - hop * step[way]

                    @pl.when(there)
                    def _(block=block, way=way):
                        on_arrival(block, way)
                        pl.when(exists[way])(functools.partial(act, block, way, False))

    barrier = pltpu.get_barrier_semaphore()
    for way in (up, down, right, left):

        @pl.when(exists[way])
        def _(way=way):
            pl.semaphore_signal(
                barrier, inc=1, device_id={"col": col + step[way]},
                device_id_type=pl.DeviceIdType.MESH,
            )

    pl.semaphore_wait(barrier, sum(there.astype(jnp.int32) for there in exists.values()))

    mine = pltpu.make_async_copy(own_ref, place(col), local_sem)
    mine.start()
    walk(
        lambda block, way: copy(block, way).wait_recv(),
        lambda block, way, own: copy(block, way, own).start(),
    )
    walk(
        lambda block, way: None,
        lambda block, way, own: copy(block, way, own).wait_send(),
    )
    mine.wait()


def gather_columns(block, columns, collective_id):
    nz, nx = CHIPS_Z, columns // CHIPS_Z
    rows, width = block.shape
    return pl.pallas_call(
        functools.partial(gather_kernel, nz, nx),
        out_shape=jax.ShapeDtypeStruct((rows, width * columns), block.dtype),
        in_specs=[pl.BlockSpec(memory_space=pl.ANY)],
        out_specs=pl.BlockSpec(memory_space=pl.ANY),
        scratch_shapes=[
            pltpu.SemaphoreType.DMA((4, columns)),
            pltpu.SemaphoreType.DMA((columns,)),
            pltpu.SemaphoreType.DMA,
        ],
        compiler_params=pltpu.CompilerParams(
            collective_id=collective_id, has_side_effects=True
        ),
        cost_estimate=pl.CostEstimate(
            flops=0, bytes_accessed=300 * rows * width * 4, transcendentals=0
        ),
        name="gather_columns_%d" % collective_id,
    )(block)


def dot(left, right, contract):
    return lax.dot_general(
        left,
        right,
        ((contract, contract) if contract == (0,) else ((1,), (0,)), ((), ())),
        precision=lax.Precision.HIGH,
        preferred_element_type=jnp.float32,
    )


def per_device(n_row, n_col, sigma_top, factor_cross, factor_inverse, block_inverse, ancestors):
    height, width = sigma_top.shape
    living_rows = ancestors.shape[0] * BLK
    chunk = living_rows // n_row
    unit = BLK
    while chunk % unit:
        unit //= 2
    row = lax.axis_index("row")

    def living_chunk(strip):
        parts = []
        for i in range(chunk // unit):
            at = row * chunk + i * unit
            start = ancestors[at // BLK] * BLK + at % BLK
            parts.append(lax.dynamic_slice(strip, (start, 0), (unit, strip.shape[1])))
        return jnp.concatenate(parts, axis=0)

    def over_row(array):
        return lax.all_gather(array, "row", axis=0, tiled=True)

    cross_strip = over_row(factor_cross)
    factor_inverse, cross_strip = lax.optimization_barrier((factor_inverse, cross_strip))
    inverse_strip = over_row(factor_inverse)
    sigma_top, inverse_strip = lax.optimization_barrier((sigma_top, inverse_strip))
    top_strip = over_row(sigma_top)

    cross = gather_columns(living_chunk(cross_strip), n_col, 1)
    update = dot(cross, inverse_strip, (1,))
    update_strip = over_row(update)
    update_wide = gather_columns(update, n_col, 2)

    shares = []
    for shift in range(n_row):
        to = lax.rem(row + shift, n_row)
        piece = lax.dynamic_slice(update_wide, (0, to * height), (chunk, height))
        if shift:
            piece = lax.ppermute(
                piece, "row", [(i, (i + shift) % n_row) for i in range(n_row)]
            )
        shares.append(piece)

    top_chunk, update_wide = lax.optimization_barrier((living_chunk(top_strip), update_wide))
    top = gather_columns(top_chunk, n_col, 3)
    top = jnp.concatenate(
        [
            lax.dynamic_slice(top, (0, ancestors[i] * BLK), (chunk, BLK))
            for i in range(ancestors.shape[0])
        ],
        axis=1,
    )
    living_cross = over_row(-dot(top, update_strip, (1,)))

    blocks = []
    for i in range(height // BLK):
        match = ancestors == row * (height // BLK) + i
        start = jnp.argmax(match).astype(jnp.int32) * BLK
        rows = lax.dynamic_slice(living_cross, (start, 0), (BLK, width))
        blocks.append(jnp.where(jnp.any(match), rows, jnp.float32(0.0)))
    sigma_cross = jnp.concatenate(blocks, axis=0)

    sigma_child = block_inverse
    for shift in range(n_row):
        source = lax.rem(row - shift + n_row, n_row)
        rows = lax.dynamic_slice(living_cross, (source * chunk, 0), (chunk, width))
        sigma_child = sigma_child - dot(shares[shift], rows, (0,))
    return (sigma_cross, sigma_child)


def solution(mesh):
    return jax.shard_map(
        functools.partial(per_device, mesh.shape["row"], mesh.shape["col"]),
        mesh=mesh,
        in_specs=(P("row", "col"), P("row", "col"), P("row", "col"), P("row", "col"), P()),
        out_specs=(P("row", "col"), P("row", "col")),
        check_vma=False,
    )
```
